768 devices in a mesh: aux: 24 (over z_lo, x), orb: 4 (over z_hi, core), rep: 8 (over y).
Axes of the slice: x: 4, y: 8, z: 12 (z_hi: 2, z_lo: 6; z = z_hi * 6 + z_lo), core: 2. Of those that a mesh axis runs over, the one named last changes fastest.
Arguments:
- tiles: bfloat16 [24, 32, 8, 1600, 128], P('aux', ('orb', 'rep')), may hold values from -0.109375 to 0.109375
- atom_of: int32 [24, 32, 8], P('aux', ('orb', 'rep')), may hold values from 0 to 31
- owner_of: int32 [24, 32, 8], P('aux', ('orb', 'rep')), may hold values from 0 to 23
- live_count: int32 [24, 32], P('aux', ('orb', 'rep')), may hold values from 1 to 8, as said below
- green: bfloat16 [2, 1280, 1280], P(None, None, 'orb'), may hold values from -0.15625 to 0.15625
- probes: bfloat16 [12, 3072], P(None, 'aux'), may hold values from -6 to 6
Outputs:
- response: float32 [12, 3072], P(None, 'aux')
The draws below stay inside these ranges and needn't reach their ends.
Inputs may be any that keep to these rules, and one draw needn't show every extreme that they name: `atom_of`: a block's orbital atom. `owner_of`: a block's auxiliary block. The first live_count slots of a list are its blocks, the rest are padding; some list is full.
All inputs are finite; a program needn't handle non-finite values.
Results may differ from the reference program's by a relative error of at most 0.0075.
Values may be sent and summed in bfloat16 or wider, within the bound.
No kernel may reach another device: no remote copies, remote signals or barrier semaphores. Data moves between devices by JAX's collectives and lax.ppermute only.
A program may use at most 64 MiB of HBM per device.

```python
import jax
import jax.numpy as jnp
from jax import lax

BA = 128
BO = 40
NB = 8
NPROBE = 12
NATM = 32
NORB = 1280
NAUXF = 3072
N_AUX = 24


def draw_live_count(key, part):
    key = jax.random.fold_in(key, 1)
    values = jax.random.randint(key, (N_AUX * NATM,), 1, NB + 1)
    picked = jax.random.randint(jax.random.fold_in(key, 2), (), 0, N_AUX * NATM)
    values = values.at[picked].set(NB)
    return values.reshape(N_AUX, NATM).astype(jnp.int32)


def set_ends(array, rng, low, high):
    dims = array.shape
    index_at = [jax.random.randint(jax.random.fold_in(rng, axis), (), 0, dims[axis]) for axis in range(len(dims))]
    array = array.at[tuple(index_at)].set(low)
    longest = dims.index(max(dims))
    index_at[longest] = (index_at[longest] + 1) % dims[longest]
    return array.at[tuple(index_at)].set(high)


def level_of(own_key, dims, cuts, least, top_value):
    factor_of = 1.0
    for dim, shards_of in cuts:
        heights = jax.random.uniform(jax.random.fold_in(jax.random.fold_in(own_key, 6), dim), (shards_of,), jnp.float32, least / len(cuts), top_value / len(cuts))
        factor_of = factor_of * jnp.repeat(jnp.exp(heights), dims[dim] // shards_of).reshape((-1,) + (1,) * (len(dims) - 1 - dim))
    return factor_of


def noise(own_key, shape, scale, most, split=(), held_as=jnp.bfloat16):
    drawn = jax.random.normal(own_key, shape, jnp.float32) * scale
    if len(split) > 0:
        drawn = level_of(own_key, shape, split, -0.22, 0.18) * drawn
    return jnp.clip(drawn, min=-most, max=most).astype(held_as)


def setup_inputs(seed: int = 0) -> dict:
    streams_of = jax.random.split(jax.random.key(seed), 7)
    return {
        "tiles": noise(streams_of[0], (N_AUX, NATM, NB, BO * BO, BA), ((BO * NB) ** -0.5 * (BA * N_AUX) ** -0.25), 0.109375, ((0, 24), (1, 32))),
        "atom_of": set_ends(jax.random.randint(streams_of[1], (N_AUX, NATM, NB), 0, NATM), jax.random.fold_in(streams_of[1], 1), 0, NATM - 1).astype(jnp.int32),
        "owner_of": set_ends(jax.random.randint(streams_of[2], (N_AUX, NATM, NB), 0, N_AUX), jax.random.fold_in(streams_of[2], 1), 0, N_AUX - 1).astype(jnp.int32),
        "live_count": draw_live_count(jax.random.fold_in(streams_of[6], 71), 0),
        "green": noise(streams_of[4], (2, NORB, NORB), NORB ** -0.5, 0.15625, ((2, 4),)),
        "probes": noise(streams_of[5], (NPROBE, NAUXF), 1.0, 6.0, ((1, 24),)),
    }


def reference(tiles, atom_of, owner_of, live_count, green, probes):
    probe_blocks = probes.astype(jnp.float32).reshape(NPROBE, N_AUX, BA)
    green_occ = green[0].astype(jnp.float32)
    green_vir = green[1].astype(jnp.float32)
    slot_ids = jnp.arange(NB, dtype=jnp.int32)
    group_ids = jnp.arange(N_AUX, dtype=jnp.int32)

    def per_atom(atom_index):
        tiles_s = tiles[:, atom_index]
        lam_atoms = atom_of[:, atom_index]
        owners = owner_of[:, atom_index]
        live_mask = (slot_ids[None, :] < live_count[:, atom_index][:, None]).astype(jnp.float32)
        chosen = jnp.take(probe_blocks, owners.reshape(-1), axis=1).reshape(NPROBE, N_AUX, NB, BA)

        def one_group(group):
            product = jnp.einsum("rbq,bkq->brk", chosen[:, group], tiles_s[group].astype(jnp.float32))
            return (product * live_mask[group][:, None, None]).astype(jnp.bfloat16)

        contracted = lax.map(one_group, group_ids)
        atom_hot = (lam_atoms[..., None] == jnp.arange(NATM, dtype=jnp.int32)).astype(jnp.float32)
        spread = jnp.einsum("gba,gbrsl->rsal", atom_hot,
                            contracted.astype(jnp.float32).reshape(N_AUX, NB, NPROBE, BO, BO))
        spread = spread.reshape(NPROBE * BO, NORB)
        w_field = jnp.dot(spread, green_vir, precision=lax.Precision.HIGHEST)
        w_half = w_field.astype(jnp.bfloat16)
        v_field = jnp.dot(w_half.astype(jnp.float32), green_occ.T,
                          precision=lax.Precision.HIGHEST).astype(jnp.bfloat16)
        picked = jnp.take(v_field.reshape(NPROBE, BO, NATM, BO), lam_atoms.reshape(-1), axis=2)
        picked = jnp.transpose(picked, (2, 0, 1, 3)).reshape(N_AUX, NB, NPROBE, BO * BO)
        owner_hot = (owners[..., None] == group_ids).astype(jnp.float32)

        def back_group(group):
            y_rows = jnp.einsum("brk,bkp->brp", picked[group].astype(jnp.float32),
                                tiles_s[group].astype(jnp.float32))
            y_rows = y_rows * live_mask[group][:, None, None]
            return jnp.einsum("bc,brp->rcp", owner_hot[group], y_rows)

        return jnp.sum(lax.map(back_group, group_ids), axis=0)

    total_rows = jnp.sum(lax.map(per_atom, jnp.arange(NATM, dtype=jnp.int32)), axis=0)
    return total_rows.reshape(NPROBE, N_AUX * BA)
```

```python
import functools

import jax
import jax.numpy as jnp
from jax import lax
from jax.experimental import pallas as pl
from jax.experimental.pallas import tpu as pltpu
from jax.sharding import Mesh
from jax.sharding import PartitionSpec as P

BO = 40
NPROBE = 12
HALVES = 2
SIG = BO // HALVES
LANE = 128
F32 = jnp.float32
BF16 = jnp.bfloat16

Z_HI = 2
AUX = ("z_lo", "x")
OUTER = ("z_hi", "z_lo", "x")
REST = ("z_hi", "core", "rep")


def iota(shape, dim):
    return lax.broadcasted_iota(jnp.int32, shape, dim)


def dot(a, b, ca, cb):
    return lax.dot_general(a, b, (((ca,), (cb,)), ((), ())), preferred_element_type=F32)


def u_kernel(owners_ref, atoms_ref, live_ref, probes_ref, tiles_ref, out_ref, acc_ref):
    b = pl.program_id(0)
    slots = pl.num_programs(0)
    slot_count = out_ref.shape[2]
    width = SIG * BO

    chosen = probes_ref[owners_ref[b]].astype(F32)
    rows = jnp.broadcast_to(chosen[:, None, :], (NPROBE, slot_count, chosen.shape[1]))
    keep = (iota(rows.shape, 1) == b) & (b < live_ref[0])
    rows = jnp.where(keep, rows, 0.0).reshape(NPROBE * slot_count, chosen.shape[1]).astype(BF16)
    part = dot(rows, tiles_ref[0], 1, 1)

    @pl.when(b == 0)
    def _():
        acc_ref[...] = part

    @pl.when(b > 0)
    def _():
        acc_ref[...] += part

    @pl.when(b == slots - 1)
    def _():
        tail = out_ref.shape[3] - width
        ids = jnp.zeros((slot_count, tail), F32)
        for k in range(slot_count):
            ids = jnp.where(iota(ids.shape, 0) == k, atoms_ref[k].astype(F32), ids)
        ids = jnp.broadcast_to(ids[None], (NPROBE, slot_count, tail)).astype(BF16)
        for h in range(HALVES):
            piece = acc_ref[:, h * width : (h + 1) * width]
            piece = piece.reshape(NPROBE, slot_count, width).astype(BF16)
            for z in range(Z_HI):
                out_ref[z, h * NPROBE : (h + 1) * NPROBE, :, :width] = piece
                out_ref[z, h * NPROBE : (h + 1) * NPROBE, :, width:] = ids


def make_u(tiles, probes_all, owners, atoms, live):
    slot_count, inner, aux_width = tiles.shape
    chunks = NPROBE * HALVES
    wide = -(-(SIG * BO + 1) // LANE) * LANE
    smem = pl.BlockSpec(memory_space=pltpu.SMEM)
    return pl.pallas_call(
        u_kernel,
        grid=(slot_count,),
        in_specs=[
            smem,
            smem,
            smem,
            pl.BlockSpec(probes_all.shape, lambda b: (0, 0, 0)),
            pl.BlockSpec((1, inner, aux_width), lambda b: (b, 0, 0)),
        ],
        out_specs=pl.BlockSpec((Z_HI, chunks, slot_count, wide), lambda b: (0, 0, 0, 0)),
        out_shape=jax.ShapeDtypeStruct((Z_HI, chunks, slot_count, wide), BF16),
        scratch_shapes=[pltpu.VMEM((NPROBE * slot_count, inner), F32)],
        compiler_params=pltpu.CompilerParams(vmem_limit_bytes=32 * 2**20),
        name="u_blocks",
    )(owners, atoms, live, probes_all, tiles)


def w_kernel(recv_ref, mine_ref, other_ref, out_ref):
    senders, slot_count, _ = recv_ref.shape
    half = senders // Z_HI
    queue = half * slot_count
    orb = mine_ref.shape[1]
    atoms = orb // BO
    width = SIG * BO

    copies = (iota((BO, orb), 1) % BO == iota((BO, orb), 0)).astype(BF16)
    own_atom = iota((atoms, orb), 1) // BO == iota((atoms, orb), 0)

    hots, spreads = [], []
    for z in range(Z_HI):
        got = recv_ref[z * half : (z + 1) * half].astype(F32).reshape(queue, recv_ref.shape[2])
        ids = got[:, width : width + 1].astype(jnp.int32)
        hot = (iota((queue, atoms), 1) == ids).astype(BF16)
        hots.append(hot)
        spread = dot(hot, got[:, :width].astype(BF16), 0, 0)
        spreads += [spread[:, s * BO : (s + 1) * BO] for s in range(SIG)]
    stacked = jnp.concatenate(spreads, axis=0)
    high = stacked.astype(BF16)
    low = (stacked - high.astype(F32)).astype(BF16)
    count = Z_HI * SIG

    def by_row(part):
        full = dot(part, copies, 1, 0).reshape(count, atoms, orb)
        return jnp.sum(jnp.where(own_atom[None], full, 0.0), axis=1).astype(BF16)

    high, low = by_row(high), by_row(low)
    v = None
    for panel in (mine_ref, other_ref):
        w = dot(high, panel[1], 1, 0) + dot(low, panel[1], 1, 0)
        part = dot(w.astype(BF16), panel[0], 1, 1)
        v = part if v is None else v + part
    spread_v = jnp.where(own_atom[None], v[:, None, :], 0.0).reshape(count * atoms, orb).astype(BF16)
    spread_v = dot(spread_v, copies, 1, 1)
    for z in range(Z_HI):
        first = z * SIG * atoms
        pieces = [spread_v[first + s * atoms : first + (s + 1) * atoms] for s in range(SIG)]
        table = jnp.concatenate(pieces, axis=1).astype(BF16)
        back = dot(hots[z], table, 1, 0).reshape(half, slot_count, width)
        out_ref[z * half : (z + 1) * half] = back.astype(BF16)


def make_v(recv, mine, other):
    senders, slot_count, _ = recv.shape
    return pl.pallas_call(
        w_kernel,
        out_shape=jax.ShapeDtypeStruct((senders, slot_count, SIG * BO), BF16),
        compiler_params=pltpu.CompilerParams(vmem_limit_bytes=56 * 2**20),
        name="w_and_v",
    )(recv, mine, other)


def y_kernel(owners_ref, live_ref, v_ref, tiles_ref, out_ref, lhs_ref):
    b = pl.program_id(0)
    slot_count = v_ref.shape[2]
    width = v_ref.shape[3]
    rows = NPROBE * slot_count

    @pl.when(b == 0)
    def _():
        out_ref[...] = jnp.zeros_like(out_ref)
        for h in range(HALVES):
            block = pl.ds(h * NPROBE, NPROBE)
            total = v_ref[0, block].astype(F32)
            for z in range(1, Z_HI):
                total = total + v_ref[z, block].astype(F32)
            lhs_ref[h] = total.reshape(rows, width).astype(BF16)

    @pl.when(b < live_ref[0])
    def _():
        y = None
        for h in range(HALVES):
            part = dot(lhs_ref[h], tiles_ref[0, h * width : (h + 1) * width, :], 1, 0)
            y = part if y is None else y + part
        y = y.reshape(NPROBE, slot_count, y.shape[1])
        y = jnp.sum(jnp.where(iota(y.shape, 1) == b, y, 0.0), axis=1)
        out_ref[owners_ref[b]] += y


def make_y(v, tiles, owners, live, groups):
    slot_count, inner, aux_width = tiles.shape
    smem = pl.BlockSpec(memory_space=pltpu.SMEM)
    return pl.pallas_call(
        y_kernel,
        grid=(slot_count,),
        in_specs=[
            smem,
            smem,
            pl.BlockSpec(v.shape, lambda b: (0, 0, 0, 0)),
            pl.BlockSpec((1, inner, aux_width), lambda b: (b, 0, 0)),
        ],
        out_specs=pl.BlockSpec((groups, NPROBE, aux_width), lambda b: (0, 0, 0)),
        out_shape=jax.ShapeDtypeStruct((groups, NPROBE, aux_width), F32),
        scratch_shapes=[pltpu.VMEM((HALVES, NPROBE * slot_count, v.shape[3]), BF16)],
        compiler_params=pltpu.CompilerParams(vmem_limit_bytes=32 * 2**20),
        name="y_by_owner",
    )(owners, live, v, tiles)


def everywhere(value, axes):
    count = lax.axis_size(axes)
    copies = jnp.broadcast_to(value[None], (count,) + value.shape)
    return lax.all_to_all(copies, axes, 0, 0)


def body(tiles, atom_of, owner_of, live_count, green, probes):
    tiles, atoms, owners, live = tiles[0, 0], atom_of[0, 0], owner_of[0, 0], live_count[0]
    slot_count = tiles.shape[0]
    groups = lax.axis_size(AUX)
    other = lax.ppermute(green, "core", [(0, 1), (1, 0)])
    probes_all = everywhere(probes, AUX)
    u = make_u(tiles, probes_all, owners, atoms, live)
    u = u.reshape((Z_HI * groups,) + u.shape[2:])
    recv = lax.all_to_all(u, OUTER, 0, 0)
    v = make_v(recv, green, other)
    v = lax.all_to_all(v, OUTER, 0, 0)
    v = v.reshape(Z_HI, groups, slot_count, SIG * BO)
    y = make_y(v, tiles, owners, live, groups)
    y = lax.all_to_all(y, AUX, 0, 0)
    y = jnp.sum(y, axis=0)
    return jnp.sum(everywhere(y, REST), axis=0)


def solution(mesh):
    aux, orb, rep = mesh.devices.shape
    x = 4
    fine = Mesh(mesh.devices.reshape(aux // x, x, Z_HI, orb // Z_HI, rep), ("z_lo", "x", "z_hi", "core", "rep"))
    orbs = ("z_hi", "core")
    return jax.shard_map(
        body,
        mesh=fine,
        in_specs=(
            P(AUX, orbs + ("rep",), None, None, None),
            P(AUX, orbs + ("rep",), None),
            P(AUX, orbs + ("rep",), None),
            P(AUX, orbs + ("rep",)),
            P(None, None, orbs),
            P(None, AUX),
        ),
        out_specs=P(None, AUX),
        check_vma=False,
    )
```

```python
import jax
import jax.numpy as jnp
from jax import lax
from jax.experimental import pallas as pl
from jax.experimental.pallas import tpu as pltpu
from jax.sharding import Mesh
from jax.sharding import PartitionSpec as P

BO = 40
NPROBE = 12
HALVES = 2
SIG = BO // HALVES
LANE = 128
F32 = jnp.float32
BF16 = jnp.bfloat16

Z_HI = 2
AUX = ("z_lo", "x")
OUTER = ("z_hi", "z_lo", "x")
LAST = ("core", "rep")


def iota(shape, dim):
    return lax.broadcasted_iota(jnp.int32, shape, dim)


def dot(a, b, ca, cb):
    return lax.dot_general(a, b, (((ca,), (cb,)), ((), ())), preferred_element_type=F32)


def u_kernel(meta_ref, probes_ref, tiles_ref, out_ref, held_ref, sems):
    slot_count, inner, aux_width = tiles_ref.shape
    width = SIG * BO
    copies = [pltpu.make_async_copy(tiles_ref.at[b], held_ref.at[b], sems.at[b]) for b in range(slot_count)]
    for copy in copies:
        copy.start()

    live = meta_ref[2 * slot_count]
    shape = (NPROBE, slot_count, aux_width)
    rows = []
    for b in range(slot_count):
        chosen = probes_ref[meta_ref[b]].astype(F32)
        keep = (iota(shape, 1) == b) & (b < live)
        part = jnp.where(keep, jnp.broadcast_to(chosen[:, None, :], shape), 0.0)
        rows.append(part.reshape(NPROBE * slot_count, aux_width).astype(BF16))
    rows = jnp.concatenate(rows, axis=1)

    tail = out_ref.shape[3] - width
    ids = jnp.zeros((slot_count, tail), F32)
    for b in range(slot_count):
        ids = jnp.where(iota(ids.shape, 0) == b, meta_ref[slot_count + b].astype(F32), ids)
    ids = jnp.broadcast_to(ids[None], (HALVES * NPROBE, slot_count, tail)).astype(BF16)
    for z in range(Z_HI):
        out_ref[z, :, :, width:] = ids

    for copy in copies:
        copy.wait()
    for h in range(HALVES):
        block = jnp.concatenate([held_ref[b, h * width : (h + 1) * width, :] for b in range(slot_count)], axis=1)
        piece = dot(rows, block, 1, 1).reshape(NPROBE, slot_count, width).astype(BF16)
        for z in range(Z_HI):
            out_ref[z, h * NPROBE : (h + 1) * NPROBE, :, :width] = piece


def make_u(tiles, probes_all, meta):
    slot_count = tiles.shape[0]
    chunks = NPROBE * HALVES
    wide = -(-(SIG * BO + 1) // LANE) * LANE
    return pl.pallas_call(
        u_kernel,
        in_specs=[
            pl.BlockSpec(memory_space=pltpu.SMEM),
            pl.BlockSpec(memory_space=pltpu.VMEM),
            pl.BlockSpec(memory_space=pltpu.HBM),
        ],
        out_specs=pl.BlockSpec(memory_space=pltpu.VMEM),
        out_shape=jax.ShapeDtypeStruct((Z_HI, chunks, slot_count, wide), BF16),
        scratch_shapes=[pltpu.VMEM(tiles.shape, BF16), pltpu.SemaphoreType.DMA((slot_count,))],
        compiler_params=pltpu.CompilerParams(vmem_limit_bytes=32 * 2**20),
        name="u_blocks",
    )(meta, probes_all, tiles)


def w_kernel(recv_ref, mine_ref, other_ref, out_ref):
    senders, slot_count, _ = recv_ref.shape
    half = senders // Z_HI
    queue = half * slot_count
    orb = mine_ref.shape[2]
    atoms = orb // BO
    width = SIG * BO

    copies = (iota((BO, orb), 1) % BO == iota((BO, orb), 0)).astype(BF16)
    own_atom = iota((atoms, orb), 1) // BO == iota((atoms, orb), 0)

    hots, spreads = [], []
    for z in range(Z_HI):
        got = recv_ref[z * half : (z + 1) * half].astype(F32).reshape(queue, recv_ref.shape[2])
        ids = got[:, width : width + 1].astype(jnp.int32)
        hot = (iota((queue, atoms), 1) == ids).astype(BF16)
        hots.append(hot)
        spread = dot(hot, got[:, :width].astype(BF16), 0, 0)
        spreads += [spread[:, s * BO : (s + 1) * BO] for s in range(SIG)]
    stacked = jnp.concatenate(spreads, axis=0)
    high = stacked.astype(BF16)
    low = (stacked - high.astype(F32)).astype(BF16)
    count = Z_HI * SIG

    def by_row(part):
        full = dot(part, copies, 1, 0).reshape(count, atoms, orb)
        return jnp.sum(jnp.where(own_atom[None], full, 0.0), axis=1).astype(BF16)

    rows = jnp.concatenate([by_row(high), by_row(low)], axis=0)
    v = None
    for panel in (mine_ref, other_ref):
        w = dot(rows, panel[1], 1, 1)
        w = w[:count] + w[count:]
        part = dot(w.astype(BF16), panel[0], 1, 0)
        v = part if v is None else v + part
    spread_v = jnp.where(own_atom[None], v[:, None, :], 0.0).reshape(count * atoms, orb).astype(BF16)
    spread_v = dot(spread_v, copies, 1, 1)
    for z in range(Z_HI):
        first = z * SIG * atoms
        pieces = [spread_v[first + s * atoms : first + (s + 1) * atoms] for s in range(SIG)]
        table = jnp.concatenate(pieces, axis=1).astype(BF16)
        back = dot(hots[z], table, 1, 0).reshape(half, slot_count, width)
        out_ref[z * half : (z + 1) * half] = back.astype(BF16)


def make_v(recv, mine, other):
    senders, slot_count, _ = recv.shape
    vmem = pl.BlockSpec(memory_space=pltpu.VMEM)
    return pl.pallas_call(
        w_kernel,
        in_specs=[vmem, vmem, vmem],
        out_specs=vmem,
        out_shape=jax.ShapeDtypeStruct((senders, slot_count, SIG * BO), BF16),
        compiler_params=pltpu.CompilerParams(vmem_limit_bytes=40 * 2**20),
        name="w_and_v",
    )(recv, mine, other)


def y_kernel(meta_ref, v_ref, tiles_ref, out_ref, sum_ref):
    slot_count = v_ref.shape[2]
    width = v_ref.shape[3]
    rows = NPROBE * slot_count
    live = meta_ref[2 * slot_count]

    sum_ref[...] = jnp.zeros_like(sum_ref)
    y = None
    for h in range(HALVES):
        block = pl.ds(h * NPROBE, NPROBE)
        total = v_ref[0, block].astype(F32)
        for z in range(1, Z_HI):
            total = total + v_ref[z, block].astype(F32)
        side = jnp.concatenate([tiles_ref[b, h * width : (h + 1) * width, :] for b in range(slot_count)], axis=1)
        part = dot(total.reshape(rows, width).astype(BF16), side, 1, 0)
        y = part if y is None else y + part
    aux_width = tiles_ref.shape[2]
    for b in range(slot_count):
        own = y[:, b * aux_width : (b + 1) * aux_width].reshape(NPROBE, slot_count, aux_width)
        keep = (iota(own.shape, 1) == b) & (b < live)
        sum_ref[meta_ref[b]] += jnp.sum(jnp.where(keep, own, 0.0), axis=1)
    for z in range(Z_HI):
        out_ref[z] = sum_ref[...].astype(BF16)


def make_y(v, tiles, meta, groups):
    aux_width = tiles.shape[2]
    vmem = pl.BlockSpec(memory_space=pltpu.VMEM)
    return pl.pallas_call(
        y_kernel,
        in_specs=[pl.BlockSpec(memory_space=pltpu.SMEM), vmem, vmem],
        out_specs=vmem,
        out_shape=jax.ShapeDtypeStruct((Z_HI, groups, NPROBE, aux_width), BF16),
        scratch_shapes=[pltpu.VMEM((groups, NPROBE, aux_width), F32)],
        compiler_params=pltpu.CompilerParams(vmem_limit_bytes=32 * 2**20),
        name="y_by_owner",
    )(meta, v, tiles)


def everywhere(value, axes):
    count = lax.axis_size(axes)
    copies = jnp.broadcast_to(value[None], (count,) + value.shape)
    return lax.all_to_all(copies, axes, 0, 0)


def body(tiles, atom_of, owner_of, live_count, green, probes):
    tiles = tiles[0, 0]
    slot_count = tiles.shape[0]
    groups = lax.axis_size(AUX)
    meta = jnp.concatenate([owner_of[0, 0], atom_of[0, 0], live_count[0]])
    mine = jnp.swapaxes(green, 1, 2)
    other = lax.ppermute(mine, "core", [(0, 1), (1, 0)])
    probes_all = everywhere(probes, AUX)
    u = make_u(tiles, probes_all, meta)
    u = u.reshape((Z_HI * groups,) + u.shape[2:])
    recv = lax.all_to_all(u, OUTER, 0, 0)
    v = make_v(recv, mine, other)
    v = lax.all_to_all(v, OUTER, 0, 0)
    v = v.reshape(Z_HI, groups, slot_count, SIG * BO)
    y = make_y(v, tiles, meta, groups)
    y = lax.all_to_all(y.reshape((Z_HI * groups,) + y.shape[2:]), OUTER, 0, 0)
    y = jnp.sum(y.astype(F32), axis=0)
    return jnp.sum(everywhere(y, LAST), axis=0)


def solution(mesh):
    aux, orb, rep = mesh.devices.shape
    x = 4
    fine = Mesh(mesh.devices.reshape(aux // x, x, Z_HI, orb // Z_HI, rep), ("z_lo", "x", "z_hi", "core", "rep"))
    orbs = ("z_hi", "core")
    return jax.shard_map(
        body,
        mesh=fine,
        in_specs=(
            P(AUX, orbs + ("rep",), None, None, None),
            P(AUX, orbs + ("rep",), None),
            P(AUX, orbs + ("rep",), None),
            P(AUX, orbs + ("rep",)),
            P(None, None, orbs),
            P(None, AUX),
        ),
        out_specs=P(None, AUX),
        check_vma=False,
    )
```

```python
import jax
import jax.numpy as jnp
from jax import lax
from jax.experimental import pallas as pl
from jax.experimental.pallas import tpu as pltpu
from jax.sharding import Mesh
from jax.sharding import PartitionSpec as P

BO = 40
NPROBE = 12
HALVES = 2
SIG = BO // HALVES
LANE = 128
F32 = jnp.float32
BF16 = jnp.bfloat16

Z_HI = 2
AUX = ("z_lo", "x")
OUTER = ("z_hi", "z_lo", "x")
LAST = ("core", "rep")


def iota(shape, dim):
    return lax.broadcasted_iota(jnp.int32, shape, dim)


def dot(a, b, ca, cb):
    return lax.dot_general(a, b, (((ca,), (cb,)), ((), ())), preferred_element_type=F32)


def turn_kernel(tiles_ref, out_ref, held_ref, sems):
    slot_count, _, aux_width = tiles_ref.shape
    width = SIG * BO
    copies = [pltpu.make_async_copy(tiles_ref.at[b], held_ref.at[b], sems.at[b]) for b in range(slot_count)]
    for copy in copies:
        copy.start()
    for b, copy in enumerate(copies):
        copy.wait()
        for h in range(HALVES):
            out_ref[h, b * aux_width : (b + 1) * aux_width, :] = held_ref[b, h * width : (h + 1) * width, :].T


def turn(tiles):
    slot_count, inner, aux_width = tiles.shape
    return pl.pallas_call(
        turn_kernel,
        in_specs=[pl.BlockSpec(memory_space=pltpu.HBM)],
        out_specs=pl.BlockSpec(memory_space=pltpu.VMEM),
        out_shape=jax.ShapeDtypeStruct((HALVES, slot_count * aux_width, inner // HALVES), BF16),
        scratch_shapes=[pltpu.VMEM(tiles.shape, BF16), pltpu.SemaphoreType.DMA((slot_count,))],
        compiler_params=pltpu.CompilerParams(vmem_limit_bytes=24 * 2**20),
        cost_estimate=pl.CostEstimate(flops=0, bytes_accessed=4 * tiles.size, transcendentals=0),
        name="turn_tiles",
    )(tiles)


def u_kernel(meta_ref, probes_ref, turned_ref, out_ref):
    slot_count = out_ref.shape[2]
    aux_width = probes_ref.shape[2]
    width = SIG * BO
    live = meta_ref[2 * slot_count]
    shape = (NPROBE, slot_count, aux_width)
    rows = []
    for b in range(slot_count):
        chosen = probes_ref[meta_ref[b]].astype(F32)
        keep = (iota(shape, 1) == b) & (b < live)
        part = jnp.where(keep, jnp.broadcast_to(chosen[:, None, :], shape), 0.0)
        rows.append(part.reshape(NPROBE * slot_count, aux_width).astype(BF16))
    rows = jnp.concatenate(rows, axis=1)

    tail = out_ref.shape[3] - width
    ids = jnp.zeros((slot_count, tail), F32)
    for b in range(slot_count):
        ids = jnp.where(iota(ids.shape, 0) == b, meta_ref[slot_count + b].astype(F32), ids)
    ids = jnp.broadcast_to(ids[None], (HALVES * NPROBE, slot_count, tail)).astype(BF16)
    for z in range(Z_HI):
        out_ref[z, :, :, width:] = ids

    for h in range(HALVES):
        piece = dot(rows, turned_ref[h], 1, 0).reshape(NPROBE, slot_count, width).astype(BF16)
        for z in range(Z_HI):
            out_ref[z, h * NPROBE : (h + 1) * NPROBE, :, :width] = piece


def make_u(turned, probes_all, meta, slot_count):
    chunks = NPROBE * HALVES
    wide = -(-(SIG * BO + 1) // LANE) * LANE
    vmem = pl.BlockSpec(memory_space=pltpu.VMEM)
    return pl.pallas_call(
        u_kernel,
        in_specs=[pl.BlockSpec(memory_space=pltpu.SMEM), vmem, vmem],
        out_specs=vmem,
        out_shape=jax.ShapeDtypeStruct((Z_HI, chunks, slot_count, wide), BF16),
        compiler_params=pltpu.CompilerParams(vmem_limit_bytes=32 * 2**20),
        name="u_blocks",
    )(meta, probes_all, turned)


def w_kernel(recv_ref, mine_ref, other_ref, out_ref):
    senders, slot_count, _ = recv_ref.shape
    half = senders // Z_HI
    queue = half * slot_count
    orb = mine_ref.shape[2]
    atoms = orb // BO
    width = SIG * BO

    copies = (iota((BO, orb), 1) % BO == iota((BO, orb), 0)).astype(BF16)
    own_atom = iota((atoms, orb), 1) // BO == iota((atoms, orb), 0)

    hots, spreads = [], []
    for z in range(Z_HI):
        got = recv_ref[z * half : (z + 1) * half].astype(F32).reshape(queue, recv_ref.shape[2])
        ids = got[:, width : width + 1].astype(jnp.int32)
        hot = (iota((queue, atoms), 1) == ids).astype(BF16)
        hots.append(hot)
        spread = dot(hot, got[:, :width].astype(BF16), 0, 0)
        spreads += [spread[:, s * BO : (s + 1) * BO] for s in range(SIG)]
    stacked = jnp.concatenate(spreads, axis=0)
    high = stacked.astype(BF16)
    low = (stacked - high.astype(F32)).astype(BF16)
    count = Z_HI * SIG

    def by_row(part):
        full = dot(part, copies, 1, 0).reshape(count, atoms, orb)
        return jnp.sum(jnp.where(own_atom[None], full, 0.0), axis=1).astype(BF16)

    rows = jnp.concatenate([by_row(high), by_row(low)], axis=0)
    v = None
    for panel in (mine_ref, other_ref):
        w = dot(rows, panel[1], 1, 1)
        w = w[:count] + w[count:]
        part = dot(w.astype(BF16), panel[0], 1, 0)
        v = part if v is None else v + part
    spread_v = jnp.where(own_atom[None], v[:, None, :], 0.0).reshape(count * atoms, orb).astype(BF16)
    spread_v = dot(spread_v, copies, 1, 1)
    for z in range(Z_HI):
        first = z * SIG * atoms
        pieces = [spread_v[first + s * atoms : first + (s + 1) * atoms] for s in range(SIG)]
        table = jnp.concatenate(pieces, axis=1).astype(BF16)
        back = dot(hots[z], table, 1, 0).reshape(half, slot_count, width)
        out_ref[z * half : (z + 1) * half] = back.astype(BF16)


def make_v(recv, mine, other):
    senders, slot_count, _ = recv.shape
    vmem = pl.BlockSpec(memory_space=pltpu.VMEM)
    return pl.pallas_call(
        w_kernel,
        in_specs=[vmem, vmem, vmem],
        out_specs=vmem,
        out_shape=jax.ShapeDtypeStruct((senders, slot_count, SIG * BO), BF16),
        compiler_params=pltpu.CompilerParams(vmem_limit_bytes=40 * 2**20),
        name="w_and_v",
    )(recv, mine, other)


def y_kernel(meta_ref, v_ref, tiles_ref, out_ref, sum_ref):
    slot_count = v_ref.shape[2]
    width = v_ref.shape[3]
    rows = NPROBE * slot_count
    live = meta_ref[2 * slot_count]

    sum_ref[...] = jnp.zeros_like(sum_ref)
    y = None
    for h in range(HALVES):
        block = pl.ds(h * NPROBE, NPROBE)
        total = v_ref[0, block].astype(F32)
        for z in range(1, Z_HI):
            total = total + v_ref[z, block].astype(F32)
        side = jnp.concatenate([tiles_ref[b, h * width : (h + 1) * width, :] for b in range(slot_count)], axis=1)
        part = dot(total.reshape(rows, width).astype(BF16), side, 1, 0)
        y = part if y is None else y + part
    aux_width = tiles_ref.shape[2]
    for b in range(slot_count):
        own = y[:, b * aux_width : (b + 1) * aux_width].reshape(NPROBE, slot_count, aux_width)
        keep = (iota(own.shape, 1) == b) & (b < live)
        sum_ref[meta_ref[b]] += jnp.sum(jnp.where(keep, own, 0.0), axis=1)
    for z in range(Z_HI):
        out_ref[z] = sum_ref[...].astype(BF16)


def make_y(v, tiles, meta, groups):
    aux_width = tiles.shape[2]
    vmem = pl.BlockSpec(memory_space=pltpu.VMEM)
    return pl.pallas_call(
        y_kernel,
        in_specs=[pl.BlockSpec(memory_space=pltpu.SMEM), vmem, vmem],
        out_specs=vmem,
        out_shape=jax.ShapeDtypeStruct((Z_HI, groups, NPROBE, aux_width), BF16),
        scratch_shapes=[pltpu.VMEM((groups, NPROBE, aux_width), F32)],
        compiler_params=pltpu.CompilerParams(vmem_limit_bytes=32 * 2**20),
        name="y_by_owner",
    )(meta, v, tiles)


def everywhere(value, axes):
    count = lax.axis_size(axes)
    copies = jnp.broadcast_to(value[None], (count,) + value.shape)
    return lax.all_to_all(copies, axes, 0, 0)


def body(tiles, atom_of, owner_of, live_count, green, probes):
    tiles = tiles[0, 0]
    slot_count = tiles.shape[0]
    groups = lax.axis_size(AUX)
    meta = jnp.concatenate([owner_of[0, 0], atom_of[0, 0], live_count[0]])
    mine = jnp.swapaxes(green, 1, 2)
    other = lax.ppermute(mine, "core", [(0, 1), (1, 0)])
    probes_all = everywhere(probes, AUX)
    probes_all, other = lax.optimization_barrier((probes_all, other))
    u = make_u(turn(tiles), probes_all, meta, slot_count)
    u = u.reshape((Z_HI * groups,) + u.shape[2:])
    recv = lax.all_to_all(u, OUTER, 0, 0)
    v = make_v(recv, mine, other)
    v = lax.all_to_all(v, OUTER, 0, 0)
    v = v.reshape(Z_HI, groups, slot_count, SIG * BO)
    y = make_y(v, tiles, meta, groups)
    y = lax.all_to_all(y.reshape((Z_HI * groups,) + y.shape[2:]), OUTER, 0, 0)
    y = jnp.sum(y.astype(F32), axis=0)
    return jnp.sum(everywhere(y, LAST), axis=0)


def solution(mesh):
    aux, orb, rep = mesh.devices.shape
    x = 4
    fine = Mesh(mesh.devices.reshape(aux // x, x, Z_HI, orb // Z_HI, rep), ("z_lo", "x", "z_hi", "core", "rep"))
    orbs = ("z_hi", "core")
    return jax.shard_map(
        body,
        mesh=fine,
        in_specs=(
            P(AUX, orbs + ("rep",), None, None, None),
            P(AUX, orbs + ("rep",), None),
            P(AUX, orbs + ("rep",), None),
            P(AUX, orbs + ("rep",)),
            P(None, None, orbs),
            P(None, AUX),
        ),
        out_specs=P(None, AUX),
        check_vma=False,
    )
```

```python
import jax
import jax.numpy as jnp
from jax import lax
from jax.experimental import pallas as pl
from jax.experimental.pallas import tpu as pltpu
from jax.sharding import Mesh
from jax.sharding import PartitionSpec as P

BO = 40
NPROBE = 12
HALVES = 2
SIG = BO // HALVES
LANE = 128
F32 = jnp.float32
BF16 = jnp.bfloat16

Z_HI = 2
AUX = ("z_lo", "x")
OUTER = ("z_hi", "z_lo", "x")
LAST = ("core", "rep")


def iota(shape, dim):
    return lax.broadcasted_iota(jnp.int32, shape, dim)


def dot(a, b, ca, cb):
    return lax.dot_general(a, b, (((ca,), (cb,)), ((), ())), preferred_element_type=F32)


def turn_kernel(tiles_ref, out_ref, held_ref, sems):
    slot_count, _, aux_width = tiles_ref.shape
    width = SIG * BO
    copies = [pltpu.make_async_copy(tiles_ref.at[b], held_ref.at[b], sems.at[b]) for b in range(slot_count)]
    for copy in copies:
        copy.start()
    for b, copy in enumerate(copies):
        copy.wait()
        for h in range(HALVES):
            out_ref[h, b * aux_width : (b + 1) * aux_width, :] = held_ref[b, h * width : (h + 1) * width, :].T


def turn(tiles):
    slot_count, inner, aux_width = tiles.shape
    return pl.pallas_call(
        turn_kernel,
        in_specs=[pl.BlockSpec(memory_space=pltpu.HBM)],
        out_specs=pl.BlockSpec(memory_space=pltpu.VMEM),
        out_shape=jax.ShapeDtypeStruct((HALVES, slot_count * aux_width, inner // HALVES), BF16),
        scratch_shapes=[pltpu.VMEM(tiles.shape, BF16), pltpu.SemaphoreType.DMA((slot_count,))],
        compiler_params=pltpu.CompilerParams(vmem_limit_bytes=24 * 2**20),
        cost_estimate=pl.CostEstimate(flops=0, bytes_accessed=4 * tiles.size, transcendentals=0),
        name="turn_tiles",
    )(tiles)


def u_kernel(meta_ref, probes_ref, turned_ref, out_ref):
    slot_count = out_ref.shape[1]
    aux_width = probes_ref.shape[2]
    width = SIG * BO
    live = meta_ref[2 * slot_count]
    shape = (NPROBE, slot_count, aux_width)
    rows = []
    for b in range(slot_count):
        chosen = probes_ref[meta_ref[b]].astype(F32)
        keep = (iota(shape, 1) == b) & (b < live)
        part = jnp.where(keep, jnp.broadcast_to(chosen[:, None, :], shape), 0.0)
        rows.append(part.reshape(NPROBE * slot_count, aux_width).astype(BF16))
    rows = jnp.concatenate(rows, axis=1)

    tail = out_ref.shape[2] - width
    ids = jnp.zeros((slot_count, tail), F32)
    for b in range(slot_count):
        ids = jnp.where(iota(ids.shape, 0) == b, meta_ref[slot_count + b].astype(F32), ids)
    ids = jnp.broadcast_to(ids[None], (HALVES * NPROBE, slot_count, tail)).astype(BF16)
    out_ref[:, :, width:] = ids

    for h in range(HALVES):
        piece = dot(rows, turned_ref[h], 1, 0).reshape(NPROBE, slot_count, width).astype(BF16)
        out_ref[h * NPROBE : (h + 1) * NPROBE, :, :width] = piece


def make_u(turned, probes_all, meta, slot_count):
    chunks = NPROBE * HALVES
    wide = -(-(SIG * BO + 1) // LANE) * LANE
    vmem = pl.BlockSpec(memory_space=pltpu.VMEM)
    return pl.pallas_call(
        u_kernel,
        in_specs=[pl.BlockSpec(memory_space=pltpu.SMEM), vmem, vmem],
        out_specs=vmem,
        out_shape=jax.ShapeDtypeStruct((chunks, slot_count, wide), BF16),
        compiler_params=pltpu.CompilerParams(vmem_limit_bytes=32 * 2**20),
        name="u_blocks",
    )(meta, probes_all, turned)


def spreader(orb):
    copies = (iota((BO, orb), 1) % BO == iota((BO, orb), 0)).astype(BF16)
    return copies, iota((orb // BO, orb), 1) // BO == iota((orb // BO, orb), 0)


def atoms_of(recv_ref, atoms):
    senders, slot_count, wide = recv_ref.shape
    ids = recv_ref[:, :, SIG * BO :].astype(F32).reshape(senders * slot_count, wide - SIG * BO)[:, :1].astype(jnp.int32)
    return (iota((senders * slot_count, atoms), 1) == ids).astype(BF16)


def through(rows, panels):
    v = None
    for panel in panels:
        w = dot(rows, panel[1], 1, 1)
        if w.shape[0] > SIG:
            w = w[:SIG] + w[SIG:]
        part = dot(w.astype(BF16), panel[0], 1, 0)
        v = part if v is None else v + part
    return v


def by_atom(recv_ref, orb, rest):
    senders, slot_count, _ = recv_ref.shape
    width = SIG * BO
    atoms = orb // BO
    copies, own_atom = spreader(orb)
    got = recv_ref[:, :, :width].astype(F32).reshape(senders * slot_count, width).astype(BF16)
    spread = dot(atoms_of(recv_ref, atoms), got, 0, 0)
    stacked = jnp.concatenate([spread[:, s * BO : (s + 1) * BO] for s in range(SIG)], axis=0)
    high = stacked.astype(BF16)

    def by_row(part):
        full = dot(part, copies, 1, 0).reshape(SIG, atoms, orb)
        return jnp.sum(jnp.where(own_atom[None], full, 0.0), axis=1).astype(BF16)

    if not rest:
        return by_row(high)
    low = (stacked - high.astype(F32)).astype(BF16)
    return jnp.concatenate([by_row(high), by_row(low)], axis=0)


def sum_kernel(recv_ref, rows_ref):
    rows_ref[...] = by_atom(recv_ref, rows_ref.shape[1], False)


def near_kernel(recv_ref, mine_ref, other_ref, out_ref):
    out_ref[...] = through(by_atom(recv_ref, out_ref.shape[1], True), (mine_ref, other_ref))


def far_kernel(rows_ref, mine_ref, other_ref, out_ref):
    out_ref[...] = through(rows_ref[...], (mine_ref, other_ref)).astype(BF16)


def back_kernel(recv_ref, near_ref, far_ref, out_ref):
    senders, slot_count, _ = recv_ref.shape
    orb = near_ref.shape[1]
    atoms = orb // BO
    copies, own_atom = spreader(orb)
    v = near_ref[...] + far_ref[...].astype(F32)
    table = jnp.where(own_atom[None], v[:, None, :], 0.0).reshape(SIG * atoms, orb).astype(BF16)
    table = dot(table, copies, 1, 1)
    table = jnp.concatenate([table[s * atoms : (s + 1) * atoms] for s in range(SIG)], axis=1).astype(BF16)
    back = dot(atoms_of(recv_ref, atoms), table, 1, 0)
    out_ref[...] = back.reshape(senders, slot_count, SIG * BO).astype(BF16)


def on_vmem(kernel, out_shape, name, *args):
    vmem = pl.BlockSpec(memory_space=pltpu.VMEM)
    return pl.pallas_call(
        kernel,
        in_specs=[vmem] * len(args),
        out_specs=vmem,
        out_shape=out_shape,
        compiler_params=pltpu.CompilerParams(vmem_limit_bytes=24 * 2**20),
        name=name,
    )(*args)


def make_rows(recv, orb):
    return on_vmem(sum_kernel, jax.ShapeDtypeStruct((SIG, orb), BF16), "u_by_atom", recv)


def make_near(recv, mine, other):
    shape = jax.ShapeDtypeStruct((SIG, mine.shape[2]), F32)
    return on_vmem(near_kernel, shape, "v_near", recv, mine, other)


def make_far(rows, mine, other):
    return on_vmem(far_kernel, jax.ShapeDtypeStruct(rows.shape, BF16), "v_far", rows, mine, other)


def make_back(recv, near, far):
    shape = jax.ShapeDtypeStruct(recv.shape[:2] + (SIG * BO,), BF16)
    return on_vmem(back_kernel, shape, "v_back", recv, near, far)


def y_kernel(meta_ref, v_ref, tiles_ref, out_ref, sum_ref):
    slot_count = v_ref.shape[1]
    width = v_ref.shape[2]
    rows = NPROBE * slot_count
    live = meta_ref[2 * slot_count]

    sum_ref[...] = jnp.zeros_like(sum_ref)
    y = None
    for h in range(HALVES):
        total = v_ref[h * NPROBE : (h + 1) * NPROBE].astype(F32)
        side = jnp.concatenate([tiles_ref[b, h * width : (h + 1) * width, :] for b in range(slot_count)], axis=1)
        part = dot(total.reshape(rows, width).astype(BF16), side, 1, 0)
        y = part if y is None else y + part
    aux_width = tiles_ref.shape[2]
    for b in range(slot_count):
        own = y[:, b * aux_width : (b + 1) * aux_width].reshape(NPROBE, slot_count, aux_width)
        keep = (iota(own.shape, 1) == b) & (b < live)
        sum_ref[meta_ref[b]] += jnp.sum(jnp.where(keep, own, 0.0), axis=1)
    for z in range(Z_HI):
        out_ref[z] = sum_ref[...].astype(BF16)


def make_y(v, tiles, meta, groups):
    aux_width = tiles.shape[2]
    vmem = pl.BlockSpec(memory_space=pltpu.VMEM)
    return pl.pallas_call(
        y_kernel,
        in_specs=[pl.BlockSpec(memory_space=pltpu.SMEM), vmem, vmem],
        out_specs=vmem,
        out_shape=jax.ShapeDtypeStruct((Z_HI, groups, NPROBE, aux_width), BF16),
        scratch_shapes=[pltpu.VMEM((groups, NPROBE, aux_width), F32)],
        compiler_params=pltpu.CompilerParams(vmem_limit_bytes=32 * 2**20),
        name="y_by_owner",
    )(meta, v, tiles)


def everywhere(value, axes):
    count = lax.axis_size(axes)
    copies = jnp.broadcast_to(value[None], (count,) + value.shape)
    return lax.all_to_all(copies, axes, 0, 0)


def mirrored(value):
    z_lo, z_hi = lax.axis_size("z_lo"), lax.axis_size("z_hi")
    pairs = [(i * z_hi + j, (z_lo - 1 - i) * z_hi + (z_hi - 1 - j)) for i in range(z_lo) for j in range(z_hi)]
    return lax.ppermute(value, ("z_lo", "z_hi"), pairs)


def swapped(value):
    return lax.ppermute(value, "core", [(0, 1), (1, 0)])


def body(tiles, atom_of, owner_of, live_count, green, probes):
    tiles = tiles[0, 0]
    slot_count = tiles.shape[0]
    groups = lax.axis_size(AUX)
    meta = jnp.concatenate([owner_of[0, 0], atom_of[0, 0], live_count[0]])
    mine = jnp.swapaxes(green, 1, 2)
    other = swapped(mine)
    probes_all, other = lax.optimization_barrier((everywhere(probes, AUX), other))
    u = make_u(turn(tiles), probes_all, meta, slot_count)
    u = lax.all_to_all(u, AUX, 0, 0)
    near = make_near(u, mine, other)
    far = mirrored(make_far(mirrored(make_rows(u, mine.shape[2])), mine, other))
    v = make_back(u, near, far)
    y = make_y(lax.all_to_all(v, AUX, 0, 0), tiles, meta, groups)
    y = lax.all_to_all(y.reshape((Z_HI * groups,) + y.shape[2:]), OUTER, 0, 0)
    y = jnp.sum(y.astype(F32), axis=0)
    return jnp.sum(everywhere(y, LAST), axis=0)


def solution(mesh):
    aux, orb, rep = mesh.devices.shape
    x = 4
    names = ("z_lo", "x", "z_hi", "core", "rep")
    fine = Mesh(mesh.devices.reshape(aux // x, x, Z_HI, orb // Z_HI, rep), names)
    orbs, atoms = names[2:4], names[2:]
    return jax.shard_map(
        body,
        mesh=fine,
        in_specs=(
            P(AUX, atoms, None, None, None),
            P(AUX, atoms, None),
            P(AUX, atoms, None),
            P(AUX, atoms),
            P(None, None, orbs),
            P(None, AUX),
        ),
        out_specs=P(None, AUX),
        check_vma=False,
    )
```

```python
import jax
import jax.numpy as jnp
from jax import lax
from jax.experimental import pallas as pl
from jax.experimental.pallas import tpu as pltpu
from jax.sharding import Mesh
from jax.sharding import PartitionSpec as P

BO = 40
NPROBE = 12
HALVES = 2
SIG = BO // HALVES
LANE = 128
F32 = jnp.float32
BF16 = jnp.bfloat16

Z_HI = 2
AUX = ("z_lo", "x")
OUTER = ("z_hi", "z_lo", "x")
LAST = ("core", "rep")


def iota(shape, dim):
    return lax.broadcasted_iota(jnp.int32, shape, dim)


def dot(a, b, ca, cb):
    return lax.dot_general(a, b, (((ca,), (cb,)), ((), ())), preferred_element_type=F32)


def turn_kernel(tiles_ref, out_ref, held_ref, sems):
    slot_count, _, aux_width = tiles_ref.shape
    width = SIG * BO
    copies = [pltpu.make_async_copy(tiles_ref.at[b], held_ref.at[b], sems.at[b]) for b in range(slot_count)]
    for copy in copies:
        copy.start()
    for b, copy in enumerate(copies):
        copy.wait()
        for h in range(HALVES):
            out_ref[h, b * aux_width : (b + 1) * aux_width, :] = held_ref[b, h * width : (h + 1) * width, :].T


def turn(tiles):
    slot_count, inner, aux_width = tiles.shape
    return pl.pallas_call(
        turn_kernel,
        in_specs=[pl.BlockSpec(memory_space=pltpu.HBM)],
        out_specs=pl.BlockSpec(memory_space=pltpu.VMEM),
        out_shape=jax.ShapeDtypeStruct((HALVES, slot_count * aux_width, inner // HALVES), BF16),
        scratch_shapes=[pltpu.VMEM(tiles.shape, BF16), pltpu.SemaphoreType.DMA((slot_count,))],
        compiler_params=pltpu.CompilerParams(vmem_limit_bytes=24 * 2**20),
        cost_estimate=pl.CostEstimate(flops=0, bytes_accessed=4 * tiles.size, transcendentals=0),
        name="turn_tiles",
    )(tiles)


def u_kernel(meta_ref, probes_ref, turned_ref, out_ref):
    slot_count = out_ref.shape[1]
    aux_width = probes_ref.shape[2]
    width = SIG * BO
    live = meta_ref[2 * slot_count]
    shape = (NPROBE, slot_count, aux_width)
    rows = []
    for b in range(slot_count):
        chosen = probes_ref[meta_ref[b]].astype(F32)
        keep = (iota(shape, 1) == b) & (b < live)
        part = jnp.where(keep, jnp.broadcast_to(chosen[:, None, :], shape), 0.0)
        rows.append(part.reshape(NPROBE * slot_count, aux_width).astype(BF16))
    rows = jnp.concatenate(rows, axis=1)

    tail = out_ref.shape[2] - width
    ids = jnp.zeros((slot_count, tail), F32)
    for b in range(slot_count):
        ids = jnp.where(iota(ids.shape, 0) == b, meta_ref[slot_count + b].astype(F32), ids)
    ids = jnp.broadcast_to(ids[None], (HALVES * NPROBE, slot_count, tail)).astype(BF16)
    out_ref[:, :, width:] = ids

    for h in range(HALVES):
        piece = dot(rows, turned_ref[h], 1, 0).reshape(NPROBE, slot_count, width).astype(BF16)
        out_ref[h * NPROBE : (h + 1) * NPROBE, :, :width] = piece


def make_u(turned, probes_all, meta, slot_count):
    chunks = NPROBE * HALVES
    wide = -(-(SIG * BO + 1) // LANE) * LANE
    vmem = pl.BlockSpec(memory_space=pltpu.VMEM)
    return pl.pallas_call(
        u_kernel,
        in_specs=[pl.BlockSpec(memory_space=pltpu.SMEM), vmem, vmem],
        out_specs=vmem,
        out_shape=jax.ShapeDtypeStruct((chunks, slot_count, wide), BF16),
        compiler_params=pltpu.CompilerParams(vmem_limit_bytes=32 * 2**20),
        name="u_blocks",
    )(meta, probes_all, turned)


def spreader(orb):
    copies = (iota((BO, orb), 1) % BO == iota((BO, orb), 0)).astype(BF16)
    return copies, iota((orb // BO, orb), 1) // BO == iota((orb // BO, orb), 0)


def atoms_of(recv_ref, atoms):
    senders, slot_count, wide = recv_ref.shape
    ids = recv_ref[:, :, SIG * BO :].astype(F32).reshape(senders * slot_count, wide - SIG * BO)[:, :1].astype(jnp.int32)
    return (iota((senders * slot_count, atoms), 1) == ids).astype(BF16)


def through(rows, panels):
    v = None
    for panel in panels:
        occ, vir = panel[0][...], panel[1][...]
        w = dot(rows, vir, 1, 1)
        if w.shape[0] > SIG:
            w = w[:SIG] + w[SIG:]
        part = dot(w.astype(BF16), occ, 1, 0)
        v = part if v is None else v + part
    return v


def by_atom(recv_ref, orb, rest):
    senders, slot_count, _ = recv_ref.shape
    width = SIG * BO
    atoms = orb // BO
    copies, own_atom = spreader(orb)
    got = recv_ref[:, :, :width].astype(F32).reshape(senders * slot_count, width).astype(BF16)
    spread = dot(atoms_of(recv_ref, atoms), got, 0, 0)
    stacked = jnp.concatenate([spread[:, s * BO : (s + 1) * BO] for s in range(SIG)], axis=0)
    high = stacked.astype(BF16)

    def by_row(part):
        full = dot(part, copies, 1, 0).reshape(SIG, atoms, orb)
        return jnp.sum(jnp.where(own_atom[None], full, 0.0), axis=1).astype(BF16)

    if not rest:
        return by_row(high)
    low = (stacked - high.astype(F32)).astype(BF16)
    return jnp.concatenate([by_row(high), by_row(low)], axis=0)


def sum_kernel(recv_ref, rows_ref):
    rows_ref[...] = by_atom(recv_ref, rows_ref.shape[1], False)


def near_kernel(recv_ref, mine_ref, occ_ref, vir_ref, out_ref):
    out_ref[...] = through(by_atom(recv_ref, out_ref.shape[1], True), ((mine_ref.at[0], mine_ref.at[1]), (occ_ref, vir_ref)))


def far_kernel(rows_ref, mine_ref, occ_ref, vir_ref, out_ref):
    out_ref[...] = through(rows_ref[...], ((mine_ref.at[0], mine_ref.at[1]), (occ_ref, vir_ref))).astype(BF16)


def back_kernel(recv_ref, near_ref, far_ref, out_ref):
    senders, slot_count, _ = recv_ref.shape
    orb = near_ref.shape[1]
    atoms = orb // BO
    copies, own_atom = spreader(orb)
    v = near_ref[...] + far_ref[...].astype(F32)
    table = jnp.where(own_atom[None], v[:, None, :], 0.0).reshape(SIG * atoms, orb).astype(BF16)
    table = dot(table, copies, 1, 1)
    table = jnp.concatenate([table[s * atoms : (s + 1) * atoms] for s in range(SIG)], axis=1).astype(BF16)
    back = dot(atoms_of(recv_ref, atoms), table, 1, 0)
    out_ref[...] = back.reshape(senders, slot_count, SIG * BO).astype(BF16)


def on_vmem(kernel, out_shape, name, *args):
    vmem = pl.BlockSpec(memory_space=pltpu.VMEM)
    return pl.pallas_call(
        kernel,
        in_specs=[vmem] * len(args),
        out_specs=vmem,
        out_shape=out_shape,
        compiler_params=pltpu.CompilerParams(vmem_limit_bytes=24 * 2**20),
        name=name,
    )(*args)


def make_rows(recv, orb):
    return on_vmem(sum_kernel, jax.ShapeDtypeStruct((SIG, orb), BF16), "u_by_atom", recv)


def make_near(recv, mine, occ, vir):
    shape = jax.ShapeDtypeStruct((SIG, mine.shape[2]), F32)
    return on_vmem(near_kernel, shape, "v_near", recv, mine, occ, vir)


def make_far(rows, mine, occ, vir):
    return on_vmem(far_kernel, jax.ShapeDtypeStruct(rows.shape, BF16), "v_far", rows, mine, occ, vir)


def make_back(recv, near, far):
    shape = jax.ShapeDtypeStruct(recv.shape[:2] + (SIG * BO,), BF16)
    return on_vmem(back_kernel, shape, "v_back", recv, near, far)


def y_kernel(meta_ref, v_ref, tiles_ref, out_ref, sum_ref):
    slot_count = v_ref.shape[1]
    width = v_ref.shape[2]
    rows = NPROBE * slot_count
    live = meta_ref[2 * slot_count]

    sum_ref[...] = jnp.zeros_like(sum_ref)
    y = None
    for h in range(HALVES):
        total = v_ref[h * NPROBE : (h + 1) * NPROBE].astype(F32)
        side = jnp.concatenate([tiles_ref[b, h * width : (h + 1) * width, :] for b in range(slot_count)], axis=1)
        part = dot(total.reshape(rows, width).astype(BF16), side, 1, 0)
        y = part if y is None else y + part
    aux_width = tiles_ref.shape[2]
    for b in range(slot_count):
        own = y[:, b * aux_width : (b + 1) * aux_width].reshape(NPROBE, slot_count, aux_width)
        keep = (iota(own.shape, 1) == b) & (b < live)
        sum_ref[meta_ref[b]] += jnp.sum(jnp.where(keep, own, 0.0), axis=1)
    for z in range(Z_HI):
        out_ref[z] = sum_ref[...].astype(BF16)


def make_y(v, tiles, meta, groups):
    aux_width = tiles.shape[2]
    vmem = pl.BlockSpec(memory_space=pltpu.VMEM)
    return pl.pallas_call(
        y_kernel,
        in_specs=[pl.BlockSpec(memory_space=pltpu.SMEM), vmem, vmem],
        out_specs=vmem,
        out_shape=jax.ShapeDtypeStruct((Z_HI, groups, NPROBE, aux_width), BF16),
        scratch_shapes=[pltpu.VMEM((groups, NPROBE, aux_width), F32)],
        compiler_params=pltpu.CompilerParams(vmem_limit_bytes=32 * 2**20),
        name="y_by_owner",
    )(meta, v, tiles)


def everywhere(value, axes):
    count = lax.axis_size(axes)
    copies = jnp.broadcast_to(value[None], (count,) + value.shape)
    return lax.all_to_all(copies, axes, 0, 0)


def beyond(value):
    z_lo, z_hi = lax.axis_size("z_lo"), lax.axis_size("z_hi")
    pairs = [(i * z_hi + j, (i + z_lo // 2) % z_lo * z_hi + (z_hi - 1 - j)) for i in range(z_lo) for j in range(z_hi)]
    return lax.ppermute(value, ("z_lo", "z_hi"), pairs)


def swapped(value):
    return lax.ppermute(value, "core", [(0, 1), (1, 0)])


def body(tiles, atom_of, owner_of, live_count, green, probes):
    tiles = tiles[0, 0]
    slot_count = tiles.shape[0]
    groups = lax.axis_size(AUX)
    meta = jnp.concatenate([owner_of[0, 0], atom_of[0, 0], live_count[0]])
    mine = jnp.swapaxes(green, 1, 2)
    vir, occ = swapped(mine[1]), swapped(mine[0])
    probes_all = everywhere(probes, AUX)
    u = make_u(turn(tiles), probes_all, meta, slot_count)
    u, vir, occ = lax.optimization_barrier((lax.all_to_all(u, AUX, 0, 0), vir, occ))
    near = make_near(u, mine, occ, vir)
    far = beyond(make_far(beyond(make_rows(u, mine.shape[2])), mine, occ, vir))
    v = make_back(u, near, far)
    y = make_y(lax.all_to_all(v, AUX, 0, 0), tiles, meta, groups)
    y = lax.all_to_all(y.reshape((Z_HI * groups,) + y.shape[2:]), OUTER, 0, 0)
    y = jnp.sum(y.astype(F32), axis=0).astype(BF16)
    return jnp.sum(everywhere(y, LAST).astype(F32), axis=0)


def solution(mesh):
    aux, orb, rep = mesh.devices.shape
    x = 4
    names = ("z_lo", "x", "z_hi", "core", "rep")
    fine = Mesh(mesh.devices.reshape(aux // x, x, Z_HI, orb // Z_HI, rep), names)
    orbs, atoms = names[2:4], names[2:]
    return jax.shard_map(
        body,
        mesh=fine,
        in_specs=(
            P(AUX, atoms, None, None, None),
            P(AUX, atoms, None),
            P(AUX, atoms, None),
            P(AUX, atoms),
            P(None, None, orbs),
            P(None, AUX),
        ),
        out_specs=P(None, AUX),
        check_vma=False,
    )
```

```python
import jax
import jax.numpy as jnp
from jax import lax
from jax.experimental import pallas as pl
from jax.experimental.pallas import tpu as pltpu
from jax.sharding import Mesh
from jax.sharding import PartitionSpec as P

BO = 40
NPROBE = 12
HALVES = 2
SIG = BO // HALVES
LANE = 128
F32 = jnp.float32
BF16 = jnp.bfloat16

Z_HI = 2
AUX = ("z_lo", "x")
OUTER = ("z_hi", "z_lo", "x")
LAST = ("core", "rep")


def iota(shape, dim):
    return lax.broadcasted_iota(jnp.int32, shape, dim)


def dot(a, b, ca, cb):
    return lax.dot_general(a, b, (((ca,), (cb,)), ((), ())), preferred_element_type=F32)


def turn_kernel(tiles_ref, out_ref, held_ref, sems):
    slot_count, _, aux_width = tiles_ref.shape
    width = SIG * BO
    copies = [pltpu.make_async_copy(tiles_ref.at[b], held_ref.at[b], sems.at[b]) for b in range(slot_count)]
    for copy in copies:
        copy.start()
    for b, copy in enumerate(copies):
        copy.wait()
        for h in range(HALVES):
            out_ref[h, b * aux_width : (b + 1) * aux_width, :] = held_ref[b, h * width : (h + 1) * width, :].T


def turn(tiles):
    slot_count, inner, aux_width = tiles.shape
    return pl.pallas_call(
        turn_kernel,
        in_specs=[pl.BlockSpec(memory_space=pltpu.HBM)],
        out_specs=pl.BlockSpec(memory_space=pltpu.VMEM),
        out_shape=jax.ShapeDtypeStruct((HALVES, slot_count * aux_width, inner // HALVES), BF16),
        scratch_shapes=[pltpu.VMEM(tiles.shape, BF16), pltpu.SemaphoreType.DMA((slot_count,))],
        compiler_params=pltpu.CompilerParams(vmem_limit_bytes=24 * 2**20),
        cost_estimate=pl.CostEstimate(flops=0, bytes_accessed=4 * tiles.size, transcendentals=0),
        name="turn_tiles",
    )(tiles)


def u_kernel(meta_ref, probes_ref, turned_ref, out_ref):
    slot_count = out_ref.shape[1]
    aux_width = probes_ref.shape[2]
    width = SIG * BO
    live = meta_ref[2 * slot_count]
    shape = (NPROBE, slot_count, aux_width)
    rows = []
    for b in range(slot_count):
        chosen = probes_ref[meta_ref[b]].astype(F32)
        keep = (iota(shape, 1) == b) & (b < live)
        part = jnp.where(keep, jnp.broadcast_to(chosen[:, None, :], shape), 0.0)
        rows.append(part.reshape(NPROBE * slot_count, aux_width).astype(BF16))
    rows = jnp.concatenate(rows, axis=1)

    tail = out_ref.shape[2] - width
    ids = jnp.zeros((slot_count, tail), F32)
    for b in range(slot_count):
        ids = jnp.where(iota(ids.shape, 0) == b, meta_ref[slot_count + b].astype(F32), ids)
    ids = jnp.broadcast_to(ids[None], (HALVES * NPROBE, slot_count, tail)).astype(BF16)
    out_ref[:, :, width:] = ids

    for h in range(HALVES):
        piece = dot(rows, turned_ref[h], 1, 0).reshape(NPROBE, slot_count, width).astype(BF16)
        out_ref[h * NPROBE : (h + 1) * NPROBE, :, :width] = piece


def make_u(turned, probes_all, meta, slot_count):
    chunks = NPROBE * HALVES
    wide = -(-(SIG * BO + 1) // LANE) * LANE
    vmem = pl.BlockSpec(memory_space=pltpu.VMEM)
    return pl.pallas_call(
        u_kernel,
        in_specs=[pl.BlockSpec(memory_space=pltpu.SMEM), vmem, vmem],
        out_specs=vmem,
        out_shape=jax.ShapeDtypeStruct((chunks, slot_count, wide), BF16),
        compiler_params=pltpu.CompilerParams(vmem_limit_bytes=32 * 2**20),
        name="u_blocks",
    )(meta, probes_all, turned)


def spreader(orb):
    copies = (iota((BO, orb), 1) % BO == iota((BO, orb), 0)).astype(BF16)
    return copies, iota((orb // BO, orb), 1) // BO == iota((orb // BO, orb), 0)


def atoms_of(recv_ref, atoms):
    senders, slot_count, wide = recv_ref.shape
    ids = recv_ref[:, :, SIG * BO :].astype(F32).reshape(senders * slot_count, wide - SIG * BO)[:, :1].astype(jnp.int32)
    return (iota((senders * slot_count, atoms), 1) == ids).astype(BF16)


def through(rows, panels):
    v = None
    for panel in panels:
        occ, vir = panel[0][...], panel[1][...]
        w = dot(rows, vir, 1, 1)
        if w.shape[0] > SIG:
            w = w[:SIG] + w[SIG:]
        part = dot(w.astype(BF16), occ, 1, 0)
        v = part if v is None else v + part
    return v


def by_atom(recv_ref, orb, rest):
    senders, slot_count, _ = recv_ref.shape
    width = SIG * BO
    atoms = orb // BO
    copies, own_atom = spreader(orb)
    got = recv_ref[:, :, :width].astype(F32).reshape(senders * slot_count, width).astype(BF16)
    spread = dot(atoms_of(recv_ref, atoms), got, 0, 0)
    stacked = jnp.concatenate([spread[:, s * BO : (s + 1) * BO] for s in range(SIG)], axis=0)
    high = stacked.astype(BF16)

    def by_row(part):
        full = dot(part, copies, 1, 0).reshape(SIG, atoms, orb)
        return jnp.sum(jnp.where(own_atom[None], full, 0.0), axis=1)

    if not rest:
        return by_row(high).astype(BF16)
    low = (stacked - high.astype(F32)).astype(BF16)
    return jnp.concatenate([by_row(high), by_row(low)], axis=0).astype(BF16)


def sum_kernel(recv_ref, rows_ref):
    rows_ref[...] = by_atom(recv_ref, rows_ref.shape[1], False)


def near_kernel(recv_ref, mine_ref, occ_ref, vir_ref, out_ref):
    out_ref[...] = through(by_atom(recv_ref, out_ref.shape[1], True), ((mine_ref.at[0], mine_ref.at[1]), (occ_ref, vir_ref)))


def far_kernel(rows_ref, mine_ref, occ_ref, vir_ref, out_ref):
    out_ref[...] = through(rows_ref[...], ((mine_ref.at[0], mine_ref.at[1]), (occ_ref, vir_ref))).astype(BF16)


def back_kernel(recv_ref, near_ref, far_ref, out_ref):
    senders, slot_count, _ = recv_ref.shape
    orb = near_ref.shape[1]
    atoms = orb // BO
    copies, own_atom = spreader(orb)
    v = near_ref[...] + far_ref[...].astype(F32)
    table = jnp.where(own_atom[None], v[:, None, :], 0.0).reshape(SIG * atoms, orb).astype(BF16)
    table = dot(table, copies, 1, 1)
    table = jnp.concatenate([table[s * atoms : (s + 1) * atoms] for s in range(SIG)], axis=1).astype(BF16)
    back = dot(atoms_of(recv_ref, atoms), table, 1, 0)
    out_ref[...] = back.reshape(senders, slot_count, SIG * BO).astype(BF16)


def on_vmem(kernel, out_shape, name, *args):
    vmem = pl.BlockSpec(memory_space=pltpu.VMEM)
    return pl.pallas_call(
        kernel,
        in_specs=[vmem] * len(args),
        out_specs=vmem,
        out_shape=out_shape,
        compiler_params=pltpu.CompilerParams(vmem_limit_bytes=24 * 2**20),
        name=name,
    )(*args)


def make_rows(recv, orb):
    return on_vmem(sum_kernel, jax.ShapeDtypeStruct((SIG, orb), BF16), "u_by_atom", recv)


def make_near(recv, mine, occ, vir):
    shape = jax.ShapeDtypeStruct((SIG, mine.shape[2]), F32)
    return on_vmem(near_kernel, shape, "v_near", recv, mine, occ, vir)


def make_far(rows, mine, occ, vir):
    return on_vmem(far_kernel, jax.ShapeDtypeStruct(rows.shape, BF16), "v_far", rows, mine, occ, vir)


def make_back(recv, near, far):
    shape = jax.ShapeDtypeStruct(recv.shape[:2] + (SIG * BO,), BF16)
    return on_vmem(back_kernel, shape, "v_back", recv, near, far)


def y_kernel(meta_ref, v_ref, tiles_ref, out_ref, sum_ref):
    slot_count = v_ref.shape[1]
    width = v_ref.shape[2]
    rows = NPROBE * slot_count
    live = meta_ref[2 * slot_count]

    sum_ref[...] = jnp.zeros_like(sum_ref)
    y = None
    for h in range(HALVES):
        total = v_ref[h * NPROBE : (h + 1) * NPROBE].astype(F32)
        side = jnp.concatenate([tiles_ref[b, h * width : (h + 1) * width, :] for b in range(slot_count)], axis=1)
        part = dot(total.reshape(rows, width).astype(BF16), side, 1, 0)
        y = part if y is None else y + part
    aux_width = tiles_ref.shape[2]
    for b in range(slot_count):
        own = y[:, b * aux_width : (b + 1) * aux_width].reshape(NPROBE, slot_count, aux_width)
        keep = (iota(own.shape, 1) == b) & (b < live)
        sum_ref[meta_ref[b]] += jnp.sum(jnp.where(keep, own, 0.0), axis=1)
    for z in range(Z_HI):
        out_ref[z] = sum_ref[...].astype(BF16)


def make_y(v, tiles, meta, groups):
    aux_width = tiles.shape[2]
    vmem = pl.BlockSpec(memory_space=pltpu.VMEM)
    return pl.pallas_call(
        y_kernel,
        in_specs=[pl.BlockSpec(memory_space=pltpu.SMEM), vmem, vmem],
        out_specs=vmem,
        out_shape=jax.ShapeDtypeStruct((Z_HI, groups, NPROBE, aux_width), BF16),
        scratch_shapes=[pltpu.VMEM((groups, NPROBE, aux_width), F32)],
        compiler_params=pltpu.CompilerParams(vmem_limit_bytes=32 * 2**20),
        name="y_by_owner",
    )(meta, v, tiles)


def everywhere(value, axes):
    count = lax.axis_size(axes)
    copies = jnp.broadcast_to(value[None], (count,) + value.shape)
    return lax.all_to_all(copies, axes, 0, 0)


def beyond(value):
    z_lo, z_hi = lax.axis_size("z_lo"), lax.axis_size("z_hi")
    pairs = [(i * z_hi + j, (i + z_lo // 2) % z_lo * z_hi + (z_hi - 1 - j)) for i in range(z_lo) for j in range(z_hi)]
    return lax.ppermute(value, ("z_lo", "z_hi"), pairs)


def swapped(value):
    return lax.ppermute(value, "core", [(0, 1), (1, 0)])


def body(tiles, atom_of, owner_of, live_count, green, probes):
    tiles = tiles[0, 0]
    slot_count = tiles.shape[0]
    groups = lax.axis_size(AUX)
    meta = jnp.concatenate([owner_of[0, 0], atom_of[0, 0], live_count[0]])
    mine = jnp.swapaxes(green, 1, 2)
    vir, occ = swapped(mine[1]), swapped(mine[0])
    probes_all = everywhere(probes, AUX)
    u = make_u(turn(tiles), probes_all, meta, slot_count)
    u, vir, occ = lax.optimization_barrier((lax.all_to_all(u, AUX, 0, 0), vir, occ))
    near = make_near(u, mine, occ, vir)
    far = beyond(make_far(beyond(make_rows(u, mine.shape[2])), mine, occ, vir))
    v = make_back(u, near, far)
    y = make_y(lax.all_to_all(v, AUX, 0, 0), tiles, meta, groups)
    y = lax.all_to_all(y.reshape((Z_HI * groups,) + y.shape[2:]), OUTER, 0, 0)
    y = jnp.sum(y.astype(F32), axis=0).astype(BF16)
    return jnp.sum(everywhere(y, LAST).astype(F32), axis=0)


def solution(mesh):
    aux, orb, rep = mesh.devices.shape
    x = 4
    names = ("z_lo", "x", "z_hi", "core", "rep")
    fine = Mesh(mesh.devices.reshape(aux // x, x, Z_HI, orb // Z_HI, rep), names)
    orbs, atoms = names[2:4], names[2:]
    return jax.shard_map(
        body,
        mesh=fine,
        in_specs=(
            P(AUX, atoms, None, None, None),
            P(AUX, atoms, None),
            P(AUX, atoms, None),
            P(AUX, atoms),
            P(None, None, orbs),
            P(None, AUX),
        ),
        out_specs=P(None, AUX),
        check_vma=False,
    )
```

```python
import jax
import jax.numpy as jnp
from jax import lax
from jax.experimental import pallas as pl
from jax.experimental.pallas import tpu as pltpu
from jax.sharding import Mesh
from jax.sharding import PartitionSpec as P

BO = 40
NPROBE = 12
HALVES = 2
SIG = BO // HALVES
LANE = 128
F32 = jnp.float32
BF16 = jnp.bfloat16

Z_HI = 2
AUX = ("z_lo", "x")
OUTER = ("z_hi", "z_lo", "x")
LAST = ("core", "rep")


def iota(shape, dim):
    return lax.broadcasted_iota(jnp.int32, shape, dim)


def dot(a, b, ca, cb):
    return lax.dot_general(a, b, (((ca,), (cb,)), ((), ())), preferred_element_type=F32)


def turn_kernel(tiles_ref, out_ref, held_ref, sems):
    slot_count, _, aux_width = tiles_ref.shape
    width = SIG * BO
    copies = [pltpu.make_async_copy(tiles_ref.at[b], held_ref.at[b], sems.at[b]) for b in range(slot_count)]
    for copy in copies:
        copy.start()
    for b, copy in enumerate(copies):
        copy.wait()
        for h in range(HALVES):
            out_ref[h, b * aux_width : (b + 1) * aux_width, :] = held_ref[b, h * width : (h + 1) * width, :].T


def turn(tiles):
    slot_count, inner, aux_width = tiles.shape
    return pl.pallas_call(
        turn_kernel,
        in_specs=[pl.BlockSpec(memory_space=pltpu.HBM)],
        out_specs=pl.BlockSpec(memory_space=pltpu.VMEM),
        out_shape=jax.ShapeDtypeStruct((HALVES, slot_count * aux_width, inner // HALVES), BF16),
        scratch_shapes=[pltpu.VMEM(tiles.shape, BF16), pltpu.SemaphoreType.DMA((slot_count,))],
        compiler_params=pltpu.CompilerParams(vmem_limit_bytes=24 * 2**20),
        cost_estimate=pl.CostEstimate(flops=0, bytes_accessed=4 * tiles.size, transcendentals=0),
        name="turn_tiles",
    )(tiles)


def u_kernel(meta_ref, probes_ref, turned_ref, out_ref):
    slot_count = out_ref.shape[1]
    aux_width = probes_ref.shape[2]
    width = SIG * BO
    live = meta_ref[2 * slot_count]
    shape = (NPROBE, slot_count, aux_width)
    rows = []
    for b in range(slot_count):
        chosen = probes_ref[meta_ref[b]].astype(F32)
        keep = (iota(shape, 1) == b) & (b < live)
        part = jnp.where(keep, jnp.broadcast_to(chosen[:, None, :], shape), 0.0)
        rows.append(part.reshape(NPROBE * slot_count, aux_width).astype(BF16))
    rows = jnp.concatenate(rows, axis=1)

    tail = out_ref.shape[2] - width
    ids = jnp.zeros((slot_count, tail), F32)
    for b in range(slot_count):
        ids = jnp.where(iota(ids.shape, 0) == b, meta_ref[slot_count + b].astype(F32), ids)
    ids = jnp.broadcast_to(ids[None], (HALVES * NPROBE, slot_count, tail)).astype(BF16)
    out_ref[:, :, width:] = ids

    for h in range(HALVES):
        piece = dot(rows, turned_ref[h], 1, 0).reshape(NPROBE, slot_count, width).astype(BF16)
        out_ref[h * NPROBE : (h + 1) * NPROBE, :, :width] = piece


def make_u(turned, probes_all, meta, slot_count):
    chunks = NPROBE * HALVES
    wide = -(-(SIG * BO + 1) // LANE) * LANE
    vmem = pl.BlockSpec(memory_space=pltpu.VMEM)
    return pl.pallas_call(
        u_kernel,
        in_specs=[pl.BlockSpec(memory_space=pltpu.SMEM), vmem, vmem],
        out_specs=vmem,
        out_shape=jax.ShapeDtypeStruct((chunks, slot_count, wide), BF16),
        compiler_params=pltpu.CompilerParams(vmem_limit_bytes=32 * 2**20),
        name="u_blocks",
    )(meta, probes_all, turned)


def spreader(orb):
    copies = (iota((BO, orb), 1) % BO == iota((BO, orb), 0)).astype(BF16)
    return copies, iota((orb // BO, orb), 1) // BO == iota((orb // BO, orb), 0)


def atoms_of(recv_ref, atoms):
    senders, slot_count, wide = recv_ref.shape
    ids = recv_ref[:, :, SIG * BO :].astype(F32).reshape(senders * slot_count, wide - SIG * BO)[:, :1].astype(jnp.int32)
    return (iota((senders * slot_count, atoms), 1) == ids).astype(BF16)


def through(rows, panels):
    v = None
    for panel in panels:
        occ, vir = panel[0][...], panel[1][...]
        w = dot(rows, vir, 1, 1)
        if w.shape[0] > SIG:
            w = w[:SIG] + w[SIG:]
        part = dot(w.astype(BF16), occ, 1, 0)
        v = part if v is None else v + part
    return v


def by_atom(recv_ref, orb, rest):
    senders, slot_count, _ = recv_ref.shape
    width = SIG * BO
    atoms = orb // BO
    copies, own_atom = spreader(orb)
    got = recv_ref[:, :, :width].astype(F32).reshape(senders * slot_count, width).astype(BF16)
    spread = dot(atoms_of(recv_ref, atoms), got, 0, 0)
    stacked = jnp.concatenate([spread[:, s * BO : (s + 1) * BO] for s in range(SIG)], axis=0)
    high = stacked.astype(BF16)

    def by_row(part):
        full = dot(part, copies, 1, 0).reshape(SIG, atoms, orb)
        return jnp.sum(jnp.where(own_atom[None], full, 0.0), axis=1)

    if not rest:
        return by_row(high).astype(BF16)
    low = (stacked - high.astype(F32)).astype(BF16)
    return jnp.concatenate([by_row(high), by_row(low)], axis=0).astype(BF16)


def sum_kernel(recv_ref, rows_ref):
    rows_ref[...] = by_atom(recv_ref, rows_ref.shape[1], False)


def near_kernel(recv_ref, mine_ref, occ_ref, vir_ref, out_ref):
    out_ref[...] = through(by_atom(recv_ref, out_ref.shape[1], True), ((mine_ref.at[0], mine_ref.at[1]), (occ_ref, vir_ref)))


def far_kernel(rows_ref, mine_ref, occ_ref, vir_ref, out_ref):
    out_ref[...] = through(rows_ref[...], ((mine_ref.at[0], mine_ref.at[1]), (occ_ref, vir_ref))).astype(BF16)


def back_kernel(recv_ref, near_ref, far_ref, out_ref):
    senders, slot_count, _ = recv_ref.shape
    orb = near_ref.shape[1]
    atoms = orb // BO
    copies, own_atom = spreader(orb)
    v = near_ref[...] + far_ref[...].astype(F32)
    table = jnp.where(own_atom[None], v[:, None, :], 0.0).reshape(SIG * atoms, orb).astype(BF16)
    table = dot(table, copies, 1, 1)
    table = jnp.concatenate([table[s * atoms : (s + 1) * atoms] for s in range(SIG)], axis=1).astype(BF16)
    back = dot(atoms_of(recv_ref, atoms), table, 1, 0)
    out_ref[...] = back.reshape(senders, slot_count, SIG * BO).astype(BF16)


def on_vmem(kernel, out_shape, name, *args):
    vmem = pl.BlockSpec(memory_space=pltpu.VMEM)
    return pl.pallas_call(
        kernel,
        in_specs=[vmem] * len(args),
        out_specs=vmem,
        out_shape=out_shape,
        compiler_params=pltpu.CompilerParams(vmem_limit_bytes=24 * 2**20),
        name=name,
    )(*args)


def make_rows(recv, orb):
    return on_vmem(sum_kernel, jax.ShapeDtypeStruct((SIG, orb), BF16), "u_by_atom", recv)


def make_near(recv, mine, occ, vir):
    shape = jax.ShapeDtypeStruct((SIG, mine.shape[2]), F32)
    return on_vmem(near_kernel, shape, "v_near", recv, mine, occ, vir)


def make_far(rows, mine, occ, vir):
    return on_vmem(far_kernel, jax.ShapeDtypeStruct(rows.shape, BF16), "v_far", rows, mine, occ, vir)


def make_back(recv, near, far):
    shape = jax.ShapeDtypeStruct(recv.shape[:2] + (SIG * BO,), BF16)
    return on_vmem(back_kernel, shape, "v_back", recv, near, far)


def y_kernel(meta_ref, v_ref, tiles_ref, out_ref, sum_ref):
    slot_count = v_ref.shape[1]
    width = v_ref.shape[2]
    rows = NPROBE * slot_count
    live = meta_ref[2 * slot_count]

    sum_ref[...] = jnp.zeros_like(sum_ref)
    y = None
    for h in range(HALVES):
        total = v_ref[h * NPROBE : (h + 1) * NPROBE].astype(F32)
        side = jnp.concatenate([tiles_ref[b, h * width : (h + 1) * width, :] for b in range(slot_count)], axis=1)
        part = dot(total.reshape(rows, width).astype(BF16), side, 1, 0)
        y = part if y is None else y + part
    aux_width = tiles_ref.shape[2]
    for b in range(slot_count):
        own = y[:, b * aux_width : (b + 1) * aux_width].reshape(NPROBE, slot_count, aux_width)
        keep = (iota(own.shape, 1) == b) & (b < live)
        sum_ref[meta_ref[b]] += jnp.sum(jnp.where(keep, own, 0.0), axis=1)
    for z in range(Z_HI):
        out_ref[z] = sum_ref[...].astype(BF16)


def make_y(v, tiles, meta, groups):
    aux_width = tiles.shape[2]
    vmem = pl.BlockSpec(memory_space=pltpu.VMEM)
    return pl.pallas_call(
        y_kernel,
        in_specs=[pl.BlockSpec(memory_space=pltpu.SMEM), vmem, vmem],
        out_specs=vmem,
        out_shape=jax.ShapeDtypeStruct((Z_HI, groups, NPROBE, aux_width), BF16),
        scratch_shapes=[pltpu.VMEM((groups, NPROBE, aux_width), F32)],
        compiler_params=pltpu.CompilerParams(vmem_limit_bytes=32 * 2**20),
        name="y_by_owner",
    )(meta, v, tiles)


def everywhere(value, axes):
    count = lax.axis_size(axes)
    copies = jnp.broadcast_to(value[None], (count,) + value.shape)
    return lax.all_to_all(copies, axes, 0, 0)


def beyond(value):
    z_lo, z_hi = lax.axis_size("z_lo"), lax.axis_size("z_hi")
    pairs = [(i * z_hi + j, (i + z_lo // 2) % z_lo * z_hi + (z_hi - 1 - j)) for i in range(z_lo) for j in range(z_hi)]
    return lax.ppermute(value, ("z_lo", "z_hi"), pairs)


def swapped(value):
    return lax.ppermute(value, "core", [(0, 1), (1, 0)])


def body(tiles, atom_of, owner_of, live_count, green, probes):
    tiles = tiles[0, 0]
    slot_count = tiles.shape[0]
    groups = lax.axis_size(AUX)
    meta = jnp.concatenate([owner_of[0, 0], atom_of[0, 0], live_count[0]])
    mine = jnp.swapaxes(green, 1, 2)
    vir = swapped(mine[1])
    probes_all = everywhere(probes, AUX)
    u = make_u(turn(tiles), probes_all, meta, slot_count)
    u, vir, own = lax.optimization_barrier((lax.all_to_all(u, AUX, 0, 0), vir, mine[0]))
    occ = swapped(own)
    near = make_near(u, mine, occ, vir)
    far = beyond(make_far(beyond(make_rows(u, mine.shape[2])), mine, occ, vir))
    v = make_back(u, near, far)
    y = make_y(lax.all_to_all(v, AUX, 0, 0), tiles, meta, groups)
    y = lax.all_to_all(y.reshape((Z_HI * groups,) + y.shape[2:]), OUTER, 0, 0)
    y = jnp.sum(y.astype(F32), axis=0).astype(BF16)
    return jnp.sum(everywhere(y, LAST).astype(F32), axis=0)


def solution(mesh):
    aux, orb, rep = mesh.devices.shape
    x = 4
    names = ("z_lo", "x", "z_hi", "core", "rep")
    fine = Mesh(mesh.devices.reshape(aux // x, x, Z_HI, orb // Z_HI, rep), names)
    orbs, atoms = names[2:4], names[2:]
    return jax.shard_map(
        body,
        mesh=fine,
        in_specs=(
            P(AUX, atoms, None, None, None),
            P(AUX, atoms, None),
            P(AUX, atoms, None),
            P(AUX, atoms),
            P(None, None, orbs),
            P(None, AUX),
        ),
        out_specs=P(None, AUX),
        check_vma=False,
    )
```
